32 devices in a mesh: groups: 2 (over x), sets: 8 (over z, y), mp: 2 (over core).
Axes of the slice: x: 2, y: 2, z: 4, core: 2. Of those that a mesh axis runs over, the one named last changes fastest.
Arguments:
- control: bfloat16 [8, 256, 2048], P('groups', 'sets'), parts along dimension 0, may hold values from -6 to 6
- line_ids: int32 [16], P(('groups', 'sets')), parts along dimension 0, may hold values from 0 to 3
- pert_ids: int32 [16], P('groups'), parts along dimension 0, may hold values from 0 to 2047
- pert_table: bfloat16 [2048, 2048], P('sets'), may hold values from -16 to 16
- blocks: int32 [16, 256], P(('groups', 'sets')), parts along dimension 0, may hold values from 0 to 3, never falling along the last dimension, each value on 1 to 128 neighbouring positions
- norm_gain: float32 [2048], replicated, may hold values from 0.1 to 1.9
- out_gain: float32 [2048], replicated, may hold values from 0.1 to 1.9
- qkv_weight: bfloat16 [2048, 3, 1024], P(None, None, 'mp'), may hold values from -1 to 1
- out_weight: bfloat16 [1024, 2048], P('mp'), may hold values from -0.75 to 0.75
- decoder: bfloat16 [2048, 12288], P('mp', 'sets'), may hold values from -0.125 to 0.125
Outputs:
- expression: bfloat16 [16, 256, 12288], P('groups', 'mp', 'sets'), parts along dimension 0
The draws below stay inside these ranges and needn't reach their ends.
There are 2 independent parts, one for each index of `groups`. The reference program is written for one: setup_inputs(seed, part) draws one part's arguments, and reference() takes and returns one part's arrays. A program takes and returns all parts, laid end to end along the dimension named above; an argument that names none is the same for every part. Nothing has to cross between parts.
Inputs may be any that keep to these rules, and one draw needn't show every extreme that they name: `blocks`: in each set the ids never fall and form 4 runs of at most 128 cells.
All inputs are finite; a program needn't handle non-finite values.
Results may differ from the reference program's by a relative error of at most 0.0058.
Values may be sent and summed in bfloat16 or wider, within the bound.
A program may use at most 128 MiB of HBM per device.

```python
import math
import jax
import jax.numpy as jnp
import numpy as np
from jax import lax

D = 2048
HEADS = 8
HD = 128
INNER = 1024
GENES = 12288
PERTS = 2048
LINES = 4
CELLS = 256
BLOCK = 128
SEGS = 4
SETS = 8


def shared_signs(key):
    direction = jnp.where(jax.random.bernoulli(jax.random.fold_in(key, 11), 0.5, (D,)), 1.0, -1.0).astype(jnp.float32)
    pattern = jnp.where(jax.random.bernoulli(jax.random.fold_in(key, 12), 0.5, (HD,)), 1.0, -1.0).astype(jnp.float32)
    chosen_head = jax.random.randint(jax.random.fold_in(key, 13), (), 0, HEADS)
    return (direction, pattern, chosen_head)


def draw_pert_table(key, part):
    direction, pattern, chosen_head = shared_signs(key)
    random_part = jnp.clip(jax.random.normal(jax.random.fold_in(key, 1), (PERTS, D), jnp.float32), -6.0, 6.0)
    strength = jnp.exp(jax.random.uniform(jax.random.fold_in(key, 2), (PERTS,), jnp.float32, math.log(2.0), math.log(6.0)))
    marked = jax.random.bernoulli(jax.random.fold_in(key, 3), 0.5, (PERTS,)).astype(jnp.float32)
    embedded = random_part + (marked * strength)[:, None] * direction[None, :]
    return embedded.astype(jnp.bfloat16)


def draw_qkv_weight(key, part):
    direction, pattern, chosen_head = shared_signs(key)
    fan_scale = 1.0 / math.sqrt(D)
    random_part = jnp.clip(jax.random.normal(jax.random.fold_in(key, 4), (D, 3, INNER), jnp.float32), -6.0, 6.0) * fan_scale
    target = 320.0
    strength = math.sqrt(target / (D * math.sqrt(HD))) * fan_scale
    head_index = jnp.arange(INNER, dtype=jnp.int32) // HD
    head_pattern = jnp.where(head_index == chosen_head, jnp.tile(pattern, HEADS), 0.0).astype(jnp.float32)
    role_mask = jnp.array([1.0, 1.0, 0.0], jnp.float32)
    weight = random_part + strength * direction[:, None, None] * role_mask[None, :, None] * head_pattern[None, None, :]
    return weight.astype(jnp.bfloat16)


def with_ends(entries, stream_key, least, high):
    shape = entries.shape
    place = [jax.random.randint(jax.random.fold_in(stream_key, axis), (), 0, shape[axis]) for axis in range(len(shape))]
    entries = entries.at[tuple(place)].set(least)
    longest = shape.index(max(shape))
    place[longest] = (place[longest] + 1) % shape[longest]
    return entries.at[tuple(place)].set(high)


def steps_of(key, dims, pieces, smallest, high):
    gain = 1.0
    for dim, shards_of in pieces:
        steps = jax.random.uniform(jax.random.fold_in(jax.random.fold_in(key, 6), dim), (shards_of,), jnp.float32, smallest / len(pieces), high / len(pieces))
        gain = gain * jnp.repeat(jnp.exp(steps), dims[dim] // shards_of).reshape((-1,) + (1,) * (len(dims) - 1 - dim))
    return gain


def profile(number_of, total, most, skew):
    portions = [(1 << 20) // math.isqrt(rank ** skew) + 1 for rank in range(2, number_of + 1)]
    surplus, counts = total - most - (number_of - 1), [1] * (number_of - 1)
    while surplus > 0:
        movable = [i for i in range(number_of - 1) if counts[i] < most]
        mass, left = sum([portions[i] for i in movable]), surplus
        for i in movable:
            addition = min(most - counts[i], max(1, left * portions[i] // mass), surplus)
            counts[i] = counts[i] + addition
            surplus = surplus - addition
    return np.array([most] + counts)


def ragged_sizes(stream_key, number_of, total, reach, skew):
    if number_of == 2:
        one = jax.random.randint(stream_key, (), max(1, total - reach), min(reach, total - 1) + 1)
        return jnp.stack([one, total - one])
    sizes = jnp.asarray(profile(number_of, total, reach, skew), jnp.int32)
    pairs = (number_of - 1) // 2
    donor, sink = sizes[1:1 + 2 * pairs:2], sizes[2:2 + 2 * pairs:2]
    room = jnp.minimum(donor - 1, reach - sink)
    moved = jax.random.randint(jax.random.fold_in(stream_key, 1), (pairs,), 0, 1 << 20) % (room + 1)
    sizes = sizes.at[1:1 + 2 * pairs:2].set(donor - moved).at[2:2 + 2 * pairs:2].set(sink + moved)
    return sizes[jax.random.permutation(jax.random.fold_in(stream_key, 2), number_of)]


def normal_values(stream_key, shape, spread, reach, split=(), kind=jnp.bfloat16):
    values = spread * jax.random.normal(stream_key, shape, jnp.float32)
    if split:
        values = values * steps_of(stream_key, shape, split, -0.22, 0.18)
    return jnp.clip(values, -reach, reach).astype(kind)


def setup_inputs(seed: int = 0, part: int = 0) -> dict:
    key_list = jax.random.split(jax.random.key(seed), 11)
    own_keys = jax.random.split(jax.random.fold_in(key_list[10], part), 11)
    return {
        "control": normal_values(own_keys[0], (LINES, CELLS, D), 1.0, 6.0, ((1, 8),)),
        "line_ids": with_ends(jax.random.randint(own_keys[1], (SETS,), 0, LINES), jax.random.fold_in(own_keys[1], 1), 0, LINES - 1).astype(jnp.int32),
        "pert_ids": with_ends(jax.random.randint(own_keys[2], (SETS,), 0, PERTS), jax.random.fold_in(own_keys[2], 1), 0, PERTS - 1).astype(jnp.int32),
        "pert_table": draw_pert_table(jax.random.fold_in(key_list[10], 71), part),
        "blocks": jax.vmap(lambda own: jnp.searchsorted(jnp.cumsum(ragged_sizes(own, SEGS, CELLS, BLOCK, 0)), jnp.arange(CELLS), side="right"))(jax.random.split(own_keys[4], SETS)).reshape((SETS, CELLS)).astype(jnp.int32),
        "norm_gain": jnp.clip(1.0 + 0.18 * jax.random.normal(key_list[5], (D,), jnp.float32), 0.1, 1.9),
        "out_gain": jnp.clip(1.0 + 0.18 * jax.random.normal(key_list[6], (D,), jnp.float32), 0.1, 1.9),
        "qkv_weight": draw_qkv_weight(jax.random.fold_in(key_list[10], 71), part),
        "out_weight": normal_values(key_list[8], (INNER, D), (INNER // 16) ** -0.5, 0.75, ((0, 2),)),
        "decoder": normal_values(key_list[9], (D, GENES), D ** -0.5, 0.125, ((0, 2), (1, 8))),
    }


def one_set(stream, set_blocks, norm_gain, out_gain, qkv_weight, out_weight, decoder):
    mean_sq = lax.optimization_barrier(jnp.mean(stream * stream, axis=1, keepdims=True))
    normed_in = (stream * lax.rsqrt(mean_sq + 1e-05) * norm_gain.astype(jnp.float32)).astype(jnp.bfloat16)
    projected = jnp.einsum('cd,dtk->ctk', normed_in.astype(jnp.float32), qkv_weight.astype(jnp.float32)).astype(jnp.bfloat16)
    projected = projected.reshape(CELLS, 3, HEADS, HD)
    queries = projected[:, 0].astype(jnp.float32)
    keys_here = projected[:, 1].astype(jnp.float32)
    values_here = projected[:, 2].astype(jnp.float32)
    scores = jnp.einsum('qhe,khe->hqk', queries, keys_here) * HD ** (-0.5)
    same_block = (set_blocks[:, None] == set_blocks[None, :])[None]
    scores = jnp.where(same_block, scores, -1e+30)
    weights = jax.nn.softmax(scores, axis=-1).astype(jnp.bfloat16)
    attended = jnp.einsum('hqk,khe->qhe', weights.astype(jnp.float32), values_here).astype(jnp.bfloat16)
    attended = attended.reshape(CELLS, INNER)
    residual = stream + jnp.dot(attended, out_weight, preferred_element_type=jnp.float32)
    mean_out = lax.optimization_barrier(jnp.mean(residual * residual, axis=1, keepdims=True))
    normed = (residual * lax.rsqrt(mean_out + 1e-05) * out_gain.astype(jnp.float32)).astype(jnp.bfloat16)
    return jnp.dot(normed, decoder, preferred_element_type=jnp.float32).astype(jnp.bfloat16)

def reference(control, line_ids, pert_ids, pert_table, blocks, norm_gain, out_gain, qkv_weight, out_weight, decoder):
    basal_rows = control[line_ids.astype(jnp.int32)].astype(jnp.float32)
    perturbed = pert_table[pert_ids.astype(jnp.int32)].astype(jnp.float32)
    stream = basal_rows + perturbed[:, None, :]

    def apply_one(packed):
        return one_set(packed[0], packed[1], norm_gain, out_gain, qkv_weight, out_weight, decoder)
    return lax.map(apply_one, (stream, blocks))
```

```python
import functools

import jax
import jax.numpy as jnp
from jax import lax
from jax.experimental import pallas as pl
from jax.experimental.pallas import tpu as pltpu
from jax.sharding import PartitionSpec as P

HD = 128
MESH = pl.DeviceIdType.MESH
MIB = 1024 * 1024


def gather_kernel(n, payload, qkv, outw, dec, cells, qkv_all, outw_all, dec_all,
                  send, recv, wsend, wrecv, local):
    nz = n // 2
    me = lax.axis_index("sets")
    m = lax.axis_index("mp")
    z, y = me // 2, me % 2
    peer = {"mp": 1 - m}
    other = {"sets": z * 2 + 1 - y}
    up = {"sets": jnp.minimum(z + 1, nz - 1) * 2 + y}
    down = {"sets": jnp.maximum(z - 1, 0) * 2 + y}

    barrier = pltpu.get_barrier_semaphore()
    pl.semaphore_signal(barrier, inc=1, device_id=peer, device_id_type=MESH)
    pl.semaphore_signal(barrier, inc=1, device_id=other, device_id_type=MESH)

    @pl.when(z < nz - 1)
    def _():
        pl.semaphore_signal(barrier, inc=1, device_id=up, device_id_type=MESH)

    @pl.when(z > 0)
    def _():
        pl.semaphore_signal(barrier, inc=1, device_id=down, device_id_type=MESH)

    own = [
        pltpu.make_async_copy(payload, cells.at[m, me], local.at[0]),
        pltpu.make_async_copy(qkv, qkv_all.at[m], local.at[1]),
        pltpu.make_async_copy(outw, outw_all.at[m], local.at[2]),
        pltpu.make_async_copy(dec, dec_all.at[m], local.at[3]),
    ]
    for copy in own:
        copy.start()

    neighbours = 2 + jnp.where(z < nz - 1, 1, 0) + jnp.where(z > 0, 1, 0)
    pl.semaphore_wait(barrier, neighbours)

    def move(src, d, target, lane):
        return pltpu.make_async_remote_copy(
            src_ref=src,
            dst_ref=cells.at[m, d],
            send_sem=send.at[d, lane],
            recv_sem=recv.at[m, d],
            device_id=target,
            device_id_type=MESH,
        )

    def landed(half, d):
        pltpu.make_async_remote_copy(
            src_ref=cells.at[half, d],
            dst_ref=cells.at[half, d],
            send_sem=send.at[d, 0],
            recv_sem=recv.at[half, d],
            device_id=peer,
            device_id_type=MESH,
        ).wait_recv()

    def each(source, act):
        for k in range(nz):
            for sign in ((0,) if k == 0 else (-1, 1)):
                at = z + sign * k

                @pl.when((at >= 0) & (at < nz))
                def _(at=at, sign=sign, k=k):
                    d = at * 2 + y
                    src = source(d, k)
                    if sign <= 0:

                        @pl.when(z < nz - 1)
                        def _():
                            act(move(src, d, up, 0))

                    if sign >= 0:

                        @pl.when(z > 0)
                        def _():
                            act(move(src, d, down, 1))

                    act(move(src, d, other, 2))
                    act(move(src, d, peer, 3))

            if k == 0:
                after_own()
            crossing(k, act)

    def crossing(k, act):
        for sign in ((0,) if k == 0 else (-1, 1)):
            at = z + sign * k

            @pl.when((at >= 0) & (at < nz))
            def _(at=at):
                d = at * 2 + 1 - y
                if act is start:
                    landed(m, d)
                act(move(cells.at[m, d], d, peer, 3))

    weights = [
        pltpu.make_async_remote_copy(
            src_ref=src,
            dst_ref=dst.at[m],
            send_sem=wsend.at[i],
            recv_sem=wrecv.at[i],
            device_id=peer,
            device_id_type=MESH,
        )
        for i, (src, dst) in enumerate(((qkv, qkv_all), (outw, outw_all), (dec, dec_all)))
    ]

    def start(copy):
        copy.start()

    def finish(copy):
        copy.wait_send()

    def source(d, k):
        if k == 0:
            return payload
        landed(m, d)
        return cells.at[m, d]

    def after_own():
        for copy in weights:
            copy.start()

    each(source, start)

    def source(d, k):
        return payload if k == 0 else cells.at[m, d]

    def after_own():
        pass

    each(source, finish)

    for d in range(n):
        landed(1 - m, d)
    for copy in weights:
        copy.wait()
    for copy in own:
        copy.wait()


def project_kernel(rows_ref, weight_ref, out_ref):
    out_ref[...] = jnp.dot(
        rows_ref[...], weight_ref[0, 0], preferred_element_type=jnp.float32
    )


def layer_kernel(pair, width, idx_ref, *refs):
    ins, (gain_ref, outw_ref, dec_ref, out_ref, att, res) = refs[: 9 * pair], refs[9 * pair :]
    half = att.shape[0] // pair
    inner = att.shape[1]
    for j in range(pair):
        c_ref, own_ref, p_ref, q_ref, k_ref, v_ref, b_ref, row_ref, col_ref = ins[9 * j : 9 * j + 9]
        p = p_ref[0]
        stream = c_ref[0].astype(jnp.float32) + p
        scale = lax.rsqrt(jnp.sum(stream * stream, axis=1, keepdims=True) / width + 1e-05)
        own = own_ref[0].astype(jnp.float32) + p
        own_scale = lax.rsqrt(jnp.sum(own * own, axis=1, keepdims=True) / width + 1e-05)
        res[j * half : (j + 1) * half, :] = own
        same = col_ref[0] == row_ref[0]
        b = b_ref[0]
        for h in range(inner // HD):
            part = slice(h * HD, (h + 1) * HD)
            q = (own_scale * (q_ref[:, part] + b[:, part])).astype(jnp.bfloat16)
            k = (scale * (k_ref[:, part] + b[:, inner + h * HD : inner + (h + 1) * HD])).astype(jnp.bfloat16)
            v = (scale * (v_ref[:, part] + b[:, 2 * inner + h * HD : 2 * inner + (h + 1) * HD])).astype(jnp.bfloat16)
            s = lax.dot_general(q, k, (((1,), (1,)), ((), ())), preferred_element_type=jnp.float32)
            s = jnp.where(same, s * HD ** (-0.5), -1e30)
            e = jnp.exp(s - jnp.max(s, axis=1, keepdims=True))
            w = (e / jnp.sum(e, axis=1, keepdims=True)).astype(jnp.bfloat16)
            att[j * half : (j + 1) * half, part] = jnp.dot(
                w, v, preferred_element_type=jnp.float32
            ).astype(jnp.bfloat16)
    residual = res[...] + jnp.dot(att[...], outw_ref[...], preferred_element_type=jnp.float32)
    norm = lax.rsqrt(jnp.sum(residual * residual, axis=1, keepdims=True) / width + 1e-05)
    normed = (residual * norm * gain_ref[...]).astype(jnp.bfloat16)
    genes = jnp.dot(normed, dec_ref[...], preferred_element_type=jnp.float32).astype(jnp.bfloat16)
    for j in range(pair):
        out_ref[j] = genes[j * half : (j + 1) * half]


def shards(n, control, line_ids, pert_ids, pert_table, blocks, norm_gain, out_gain,
           qkv_weight, out_weight, decoder):
    lines, cells_here, width = control.shape
    cell_count = blocks.shape[1]
    sets = pert_ids.shape[0]
    inner_here = qkv_weight.shape[2]
    inner = 2 * inner_here
    genes = decoder.shape[1]
    hw = width // 2
    half = cell_count // 2
    m = lax.axis_index("mp")

    table_rows = pert_table.shape[0]
    offset = lax.axis_index("sets") * table_rows
    padded = -(-sets // 16) * 16
    ids = jnp.pad(pert_ids, (0, padded - sets), constant_values=-1)
    onehot = (
        ids[:, None] == offset + jnp.arange(table_rows, dtype=jnp.int32)[None, :]
    ).astype(jnp.bfloat16)
    table_half = lax.dynamic_slice_in_dim(pert_table, m * hw, hw, 1)
    rows = jnp.dot(onehot, table_half, preferred_element_type=jnp.float32).astype(jnp.bfloat16)
    extra = jnp.zeros((16, hw), jnp.bfloat16)
    extra = extra.at[0].set(line_ids[0].astype(jnp.bfloat16))
    extra = extra.at[1, :cell_count].set(blocks[0].astype(jnp.bfloat16))
    control_half = lax.dynamic_slice_in_dim(control, m * hw, hw, 2).reshape(lines * cells_here, hw)
    payload = jnp.concatenate([control_half, rows, extra], axis=0)
    height = payload.shape[0]

    any_spec = pl.BlockSpec(memory_space=pl.ANY)
    qkv_t = jnp.transpose(qkv_weight, (1, 0, 2))
    gathered, qkv_all, outw_all, dec_all = pl.pallas_call(
        functools.partial(gather_kernel, n),
        out_shape=(
            jax.ShapeDtypeStruct((2, n, height, hw), jnp.bfloat16),
            jax.ShapeDtypeStruct((2,) + qkv_t.shape, jnp.bfloat16),
            jax.ShapeDtypeStruct((2,) + out_weight.shape, jnp.bfloat16),
            jax.ShapeDtypeStruct((2,) + decoder.shape, jnp.bfloat16),
        ),
        in_specs=[any_spec] * 4,
        out_specs=(any_spec,) * 4,
        scratch_shapes=[
            pltpu.SemaphoreType.DMA((n, 4)),
            pltpu.SemaphoreType.DMA((2, n)),
            pltpu.SemaphoreType.DMA((3,)),
            pltpu.SemaphoreType.DMA((3,)),
            pltpu.SemaphoreType.DMA((4,)),
        ],
        compiler_params=pltpu.CompilerParams(
            collective_id=0, has_side_effects=True, vmem_limit_bytes=16 * MIB
        ),
    )(payload, qkv_t, out_weight, decoder)

    count = lines * cells_here
    cells = gathered[:, :, :count].reshape(2, n, lines, cells_here, hw)
    cells = jnp.transpose(cells, (2, 1, 3, 0, 4)).reshape(lines, cell_count, width)
    pert = jnp.sum(gathered[:, :, count : count + sets].astype(jnp.float32), axis=1)
    pert = jnp.transpose(pert, (1, 0, 2)).reshape(sets, width)
    line_all = gathered[0, :, count + padded, 0].astype(jnp.int32)
    blocks_all = gathered[0, :, count + padded + 1, :cell_count].astype(jnp.float32)
    own_blocks = lax.dynamic_slice_in_dim(blocks_all, m * half, half, 1)

    scaled = pert * norm_gain
    high = scaled.astype(jnp.bfloat16)
    low = (scaled - high.astype(jnp.float32)).astype(jnp.bfloat16)
    scaled_cells = (cells.astype(jnp.float32) * norm_gain).astype(jnp.bfloat16)
    lhs = jnp.concatenate([scaled_cells.reshape(-1, width), high, low], axis=0)
    projected = pl.pallas_call(
        project_kernel,
        grid=(6,),
        out_shape=jax.ShapeDtypeStruct((lhs.shape[0], 3 * inner), jnp.float32),
        in_specs=[
            pl.BlockSpec(lhs.shape, lambda i: (0, 0)),
            pl.BlockSpec((1, 1, width, inner_here), lambda i: (i % 2, i // 2, 0, 0)),
        ],
        out_specs=pl.BlockSpec((lhs.shape[0], inner_here), lambda i: (0, i)),
        compiler_params=pltpu.CompilerParams(vmem_limit_bytes=50 * MIB),
    )(lhs, qkv_all)
    base = lines * cell_count
    bias = projected[base : base + sets] + projected[base + sets : base + 2 * sets]

    pair = 2
    specs = []
    args = []
    for j in range(pair):
        specs += [
            pl.BlockSpec((1, cell_count, width), lambda i, r, j=j: (r[i * pair + j], 0, 0)),
            pl.BlockSpec((1, half, width), lambda i, r, j=j: (r[i * pair + j], r[sets], 0)),
            pl.BlockSpec((1, 1, width), lambda i, r, j=j: (i * pair + j, 0, 0)),
            pl.BlockSpec((half, inner), lambda i, r, j=j: (r[i * pair + j] * 2 + r[sets], 0)),
            pl.BlockSpec((cell_count, inner), lambda i, r, j=j: (r[i * pair + j], 1)),
            pl.BlockSpec((cell_count, inner), lambda i, r, j=j: (r[i * pair + j], 2)),
            pl.BlockSpec((1, 1, 3 * inner), lambda i, r, j=j: (i * pair + j, 0, 0)),
            pl.BlockSpec((1, 1, cell_count), lambda i, r, j=j: (i * pair + j, 0, 0)),
            pl.BlockSpec((1, half, 1), lambda i, r, j=j: (i * pair + j, 0, 0)),
        ]
        args += [
            cells, cells, pert[:, None, :], projected, projected, projected,
            bias[:, None, :], blocks_all[:, None, :], own_blocks[:, :, None],
        ]
    specs += [
        pl.BlockSpec((1, width), lambda i, r: (0, 0)),
        pl.BlockSpec((inner, width), lambda i, r: (0, 0), pipeline_mode=pl.Buffered(1)),
        pl.BlockSpec((width, genes), lambda i, r: (0, 0), pipeline_mode=pl.Buffered(1)),
    ]
    args += [out_gain[None], outw_all.reshape(inner, width), dec_all.reshape(width, genes)]
    return pl.pallas_call(
        functools.partial(layer_kernel, pair, width),
        grid_spec=pltpu.PrefetchScalarGridSpec(
            num_scalar_prefetch=1,
            grid=(sets // pair,),
            in_specs=specs,
            out_specs=pl.BlockSpec((pair, half, genes), lambda i, r: (i, 0, 0)),
            scratch_shapes=[
                pltpu.VMEM((pair * half, inner), jnp.bfloat16),
                pltpu.VMEM((pair * half, width), jnp.float32),
            ],
        ),
        out_shape=jax.ShapeDtypeStruct((sets, half, genes), jnp.bfloat16),
        compiler_params=pltpu.CompilerParams(vmem_limit_bytes=56 * MIB),
    )(jnp.concatenate([line_all, m[None].astype(jnp.int32)]), *args)


def solution(mesh):
    placed = (
        P("groups", "sets", None),
        P(("groups", "sets")),
        P("groups"),
        P("sets", None),
        P(("groups", "sets"), None),
        P(),
        P(),
        P(None, None, "mp"),
        P("mp", None),
        P("mp", "sets"),
    )
    return jax.shard_map(
        functools.partial(shards, mesh.shape["sets"]),
        mesh=mesh, in_specs=placed, out_specs=P("groups", "mp", "sets"), check_vma=False,
    )
```

```python
import functools

import jax
import jax.numpy as jnp
from jax import lax
from jax.experimental import pallas as pl
from jax.experimental.pallas import tpu as pltpu
from jax.sharding import PartitionSpec as P

HD = 128
MESH = pl.DeviceIdType.MESH
MIB = 1024 * 1024


def gather_kernel(n, payload, qkv, outw, dec, cells, qkv_all, outw_all, dec_all,
                  send, recv, wsend, wrecv, local):
    nz = n // 2
    me = lax.axis_index("sets")
    m = lax.axis_index("mp")
    z, y = me // 2, me % 2
    peer = {"mp": 1 - m}
    other = {"sets": z * 2 + 1 - y}
    up = {"sets": jnp.minimum(z + 1, nz - 1) * 2 + y}
    down = {"sets": jnp.maximum(z - 1, 0) * 2 + y}

    barrier = pltpu.get_barrier_semaphore()
    pl.semaphore_signal(barrier, inc=1, device_id=peer, device_id_type=MESH)
    pl.semaphore_signal(barrier, inc=1, device_id=other, device_id_type=MESH)

    @pl.when(z < nz - 1)
    def _():
        pl.semaphore_signal(barrier, inc=1, device_id=up, device_id_type=MESH)

    @pl.when(z > 0)
    def _():
        pl.semaphore_signal(barrier, inc=1, device_id=down, device_id_type=MESH)

    own = [
        pltpu.make_async_copy(payload, cells.at[m, me], local.at[0]),
        pltpu.make_async_copy(qkv, qkv_all.at[m], local.at[1]),
        pltpu.make_async_copy(outw, outw_all.at[m], local.at[2]),
        pltpu.make_async_copy(dec, dec_all.at[m], local.at[3]),
    ]
    for copy in own:
        copy.start()

    neighbours = 2 + jnp.where(z < nz - 1, 1, 0) + jnp.where(z > 0, 1, 0)
    pl.semaphore_wait(barrier, neighbours)

    def move(src, d, target, lane):
        return pltpu.make_async_remote_copy(
            src_ref=src,
            dst_ref=cells.at[m, d],
            send_sem=send.at[d, lane],
            recv_sem=recv.at[m, d],
            device_id=target,
            device_id_type=MESH,
        )

    def landed(half, d):
        pltpu.make_async_remote_copy(
            src_ref=cells.at[half, d],
            dst_ref=cells.at[half, d],
            send_sem=send.at[d, 0],
            recv_sem=recv.at[half, d],
            device_id=peer,
            device_id_type=MESH,
        ).wait_recv()

    def each(source, act):
        for k in range(nz):
            for sign in ((0,) if k == 0 else (-1, 1)):
                at = z + sign * k

                @pl.when((at >= 0) & (at < nz))
                def _(at=at, sign=sign, k=k):
                    d = at * 2 + y
                    src = source(d, k)
                    if sign <= 0:

                        @pl.when(z < nz - 1)
                        def _():
                            act(move(src, d, up, 0))

                    if sign >= 0:

                        @pl.when(z > 0)
                        def _():
                            act(move(src, d, down, 1))

                    act(move(src, d, other, 2))
                    act(move(src, d, peer, 3))

            if k == 0:
                after_own()
            crossing(k, act)

    def crossing(k, act):
        for sign in ((0,) if k == 0 else (-1, 1)):
            at = z + sign * k

            @pl.when((at >= 0) & (at < nz))
            def _(at=at):
                d = at * 2 + 1 - y
                if act is start:
                    landed(m, d)
                act(move(cells.at[m, d], d, peer, 3))

    weights = [
        pltpu.make_async_remote_copy(
            src_ref=src,
            dst_ref=dst.at[m],
            send_sem=wsend.at[i],
            recv_sem=wrecv.at[i],
            device_id=peer,
            device_id_type=MESH,
        )
        for i, (src, dst) in enumerate(((qkv, qkv_all), (outw, outw_all), (dec, dec_all)))
    ]

    def start(copy):
        copy.start()

    def finish(copy):
        copy.wait_send()

    def source(d, k):
        if k == 0:
            return payload
        landed(m, d)
        return cells.at[m, d]

    def after_own():
        for copy in weights:
            copy.start()

    each(source, start)

    def source(d, k):
        return payload if k == 0 else cells.at[m, d]

    def after_own():
        pass

    each(source, finish)

    for d in range(n):
        landed(1 - m, d)
    for copy in weights:
        copy.wait()
    for copy in own:
        copy.wait()


def layer_kernel(n, lines, sets, pair, width, idx_ref, gath_ref, weight_ref, in_gain_ref,
                 gain_ref, outw_hbm, dec_hbm, out_ref, cells, lhs, pert, proj_q, proj_kv, bias,
                 labels, att, res, outw, dec, sem):
    i = pl.program_id(0)
    m = idx_ref[sets]
    cell_count = cells.shape[1]
    half = cell_count // 2
    here = cell_count // n
    hw = width // 2
    inner_here = proj_q.shape[3]
    count = lines * here
    base = lines * cell_count
    padded = -(-sets // 16) * 16
    fetch = [
        pltpu.make_async_copy(outw_hbm, outw, sem.at[0]),
        pltpu.make_async_copy(dec_hbm, dec, sem.at[1]),
    ]

    @pl.when(i == 0)
    def _():
        for copy in fetch:
            copy.start()
        for h in range(2):
            cols = slice(h * hw, (h + 1) * hw)
            gain = in_gain_ref[:, cols]
            total = jnp.zeros((sets, hw), jnp.float32)
            for d in range(n):
                for l in range(lines):
                    block = gath_ref[h, d, l * here : (l + 1) * here, :]
                    cells[l, d * here : (d + 1) * here, cols] = block
                    at = l * cell_count + d * here
                    lhs[at : at + here, cols] = (block.astype(jnp.float32) * gain).astype(jnp.bfloat16)
                total += gath_ref[h, d, count : count + padded, :].astype(jnp.float32)[:sets]
            for s in range(sets):
                pert[s, :, cols] = total[s : s + 1]
            scaled = total * gain
            high = scaled.astype(jnp.bfloat16).astype(jnp.float32)
            lhs[base : base + 2 * sets, cols] = jnp.concatenate(
                [high, scaled - high], axis=0
            ).astype(jnp.bfloat16)
        for d in range(n):
            slab = gath_ref[0, d, count + padded : count + padded + 16, :cell_count]
            labels[d] = slab.astype(jnp.float32)[1:2]

    def put_bias(terms):
        total = terms[:sets] + terms[sets:]
        for s in range(sets):
            bias[i, s] = total[s : s + 1]

    @pl.when(i < 2)
    def _():
        rows = [
            lhs[pl.ds(pl.multiple_of(l * cell_count + m * half, half), half), :]
            for l in range(lines)
        ]
        rows = jnp.concatenate(rows + [lhs[base:, :]], axis=0)
        q = jnp.dot(rows, weight_ref[0, 0], preferred_element_type=jnp.float32)
        for l in range(lines):
            proj_q[i, l] = q[l * half : (l + 1) * half]
        put_bias(q[lines * half :])

    @pl.when((i >= 2) & (i < 6))
    def _():
        kv = jnp.dot(lhs[...], weight_ref[0, 0], preferred_element_type=jnp.float32)
        for l in range(lines):
            proj_kv[i - 2, l] = kv[l * cell_count : (l + 1) * cell_count]
        put_bias(kv[base:])

    @pl.when(i == 6)
    def _():
        for copy in fetch:
            copy.wait()

    @pl.when(i >= 6)
    def _():
        for j in range(pair):
            s_at = (i - 6) * pair + j
            line = idx_ref[s_at]
            p = pert[s_at]
            stream = cells[line].astype(jnp.float32) + p
            scale = lax.rsqrt(jnp.sum(stream * stream, axis=1, keepdims=True) / width + 1e-05)
            own = cells[line, pl.ds(pl.multiple_of(m * half, half), half), :].astype(jnp.float32) + p
            own_scale = lax.rsqrt(jnp.sum(own * own, axis=1, keepdims=True) / width + 1e-05)
            res[j * half : (j + 1) * half, :] = own
            member = (
                labels[s_at]
                == lax.broadcasted_iota(jnp.int32, (8, cell_count), 0).astype(jnp.float32)
            ).astype(jnp.float32)
            mine = jnp.where(m == 0, member[:, :half], member[:, half:])
            same = lax.dot_general(
                mine, member, (((0,), (0,)), ((), ())), preferred_element_type=jnp.float32
            ) > 0.5
            for hh in range(2):
                q_all = (own_scale * (proj_q[hh, line] + bias[hh, s_at])).astype(jnp.bfloat16)
                k_all = (scale * (proj_kv[hh, line] + bias[2 + hh, s_at])).astype(jnp.bfloat16)
                v_all = (scale * (proj_kv[2 + hh, line] + bias[4 + hh, s_at])).astype(jnp.bfloat16)
                heads = inner_here // HD
                parts = [slice(h * HD, (h + 1) * HD) for h in range(heads)]
                scores = [
                    lax.dot_general(
                        q_all[:, part], k_all[:, part], (((1,), (1,)), ((), ())),
                        preferred_element_type=jnp.float32,
                    )
                    for part in parts
                ]
                scores = [jnp.where(same, s * HD ** (-0.5), -1e30) for s in scores]
                exps = [jnp.exp(s - jnp.max(s, axis=1, keepdims=True)) for s in scores]
                weights = [
                    (e * (1.0 / jnp.sum(e, axis=1, keepdims=True))).astype(jnp.bfloat16) for e in exps
                ]
                for h in range(heads):
                    at = hh * inner_here + h * HD
                    att[j * half : (j + 1) * half, at : at + HD] = jnp.dot(
                        weights[h], v_all[:, parts[h]], preferred_element_type=jnp.float32
                    ).astype(jnp.bfloat16)
        residual = res[...] + jnp.dot(att[...], outw[...], preferred_element_type=jnp.float32)
        norm = lax.rsqrt(jnp.sum(residual * residual, axis=1, keepdims=True) / width + 1e-05)
        normed = (residual * norm * gain_ref[...]).astype(jnp.bfloat16)
        genes = jnp.dot(normed, dec[...], preferred_element_type=jnp.float32).astype(jnp.bfloat16)
        for j in range(pair):
            out_ref[j] = genes[j * half : (j + 1) * half]


def shards(n, control, line_ids, pert_ids, pert_table, blocks, norm_gain, out_gain,
           qkv_weight, out_weight, decoder):
    lines, cells_here, width = control.shape
    cell_count = blocks.shape[1]
    sets = pert_ids.shape[0]
    inner_here = qkv_weight.shape[2]
    inner = 2 * inner_here
    genes = decoder.shape[1]
    hw = width // 2
    half = cell_count // 2
    m = lax.axis_index("mp")

    table_rows = pert_table.shape[0]
    offset = lax.axis_index("sets") * table_rows
    padded = -(-sets // 16) * 16
    ids = jnp.pad(pert_ids, (0, padded - sets), constant_values=-1)
    onehot = (
        ids[:, None] == offset + jnp.arange(table_rows, dtype=jnp.int32)[None, :]
    ).astype(jnp.bfloat16)
    table_half = lax.dynamic_slice_in_dim(pert_table, m * hw, hw, 1)
    rows = jnp.dot(onehot, table_half, preferred_element_type=jnp.float32).astype(jnp.bfloat16)
    extra = jnp.zeros((16, hw), jnp.bfloat16)
    extra = extra.at[0].set(line_ids[0].astype(jnp.bfloat16))
    extra = extra.at[1, :cell_count].set(blocks[0].astype(jnp.bfloat16))
    control_half = lax.dynamic_slice_in_dim(control, m * hw, hw, 2).reshape(lines * cells_here, hw)
    payload = jnp.concatenate([control_half, rows, extra], axis=0)
    height = payload.shape[0]

    any_spec = pl.BlockSpec(memory_space=pl.ANY)
    qkv_t = jnp.transpose(qkv_weight, (1, 0, 2))
    gathered, qkv_all, outw_all, dec_all = pl.pallas_call(
        functools.partial(gather_kernel, n),
        out_shape=(
            jax.ShapeDtypeStruct((2, n, height, hw), jnp.bfloat16),
            jax.ShapeDtypeStruct((2,) + qkv_t.shape, jnp.bfloat16),
            jax.ShapeDtypeStruct((2,) + out_weight.shape, jnp.bfloat16),
            jax.ShapeDtypeStruct((2,) + decoder.shape, jnp.bfloat16),
        ),
        in_specs=[any_spec] * 4,
        out_specs=(any_spec,) * 4,
        scratch_shapes=[
            pltpu.SemaphoreType.DMA((n, 4)),
            pltpu.SemaphoreType.DMA((2, n)),
            pltpu.SemaphoreType.DMA((3,)),
            pltpu.SemaphoreType.DMA((3,)),
            pltpu.SemaphoreType.DMA((4,)),
        ],
        compiler_params=pltpu.CompilerParams(
            collective_id=0, has_side_effects=True, vmem_limit_bytes=60 * MIB
        ),
    )(payload, qkv_t, out_weight, decoder)

    line_all = gathered[0, :, lines * cells_here + padded, 0].astype(jnp.int32)
    pair = 2
    rows_all = lines * cell_count + 2 * sets
    return pl.pallas_call(
        functools.partial(layer_kernel, n, lines, sets, pair, width),
        grid_spec=pltpu.PrefetchScalarGridSpec(
            num_scalar_prefetch=1,
            grid=(6 + sets // pair,),
            in_specs=[
                pl.BlockSpec(
                    gathered.shape, lambda i, r: (0, 0, 0, 0), pipeline_mode=pl.Buffered(1)
                ),
                pl.BlockSpec(
                    (1, 1, width, inner_here),
                    lambda i, r: (jnp.minimum(i, 5) % 2, jnp.minimum(i, 5) // 2, 0, 0),
                ),
                pl.BlockSpec((1, width), lambda i, r: (0, 0)),
                pl.BlockSpec((1, width), lambda i, r: (0, 0)),
                any_spec,
                any_spec,
            ],
            out_specs=pl.BlockSpec(
                (pair, half, genes), lambda i, r: (jnp.maximum(i - 6, 0), 0, 0)
            ),
            scratch_shapes=[
                pltpu.VMEM((lines, cell_count, width), jnp.bfloat16),
                pltpu.VMEM((rows_all, width), jnp.bfloat16),
                pltpu.VMEM((sets, 1, width), jnp.float32),
                pltpu.VMEM((2, lines, half, inner_here), jnp.float32),
                pltpu.VMEM((4, lines, cell_count, inner_here), jnp.float32),
                pltpu.VMEM((6, sets, 1, inner_here), jnp.float32),
                pltpu.VMEM((sets, 1, cell_count), jnp.float32),
                pltpu.VMEM((pair * half, inner), jnp.bfloat16),
                pltpu.VMEM((pair * half, width), jnp.float32),
                pltpu.VMEM((inner, width), jnp.bfloat16),
                pltpu.VMEM((width, genes), jnp.bfloat16),
                pltpu.SemaphoreType.DMA((2,)),
            ],
        ),
        out_shape=jax.ShapeDtypeStruct((sets, half, genes), jnp.bfloat16),
        compiler_params=pltpu.CompilerParams(vmem_limit_bytes=60 * MIB),
    )(
        jnp.concatenate([line_all, m[None].astype(jnp.int32)]),
        gathered, qkv_all, norm_gain[None], out_gain[None],
        outw_all.reshape(inner, width), dec_all.reshape(width, genes),
    )


def solution(mesh):
    placed = (
        P("groups", "sets", None),
        P(("groups", "sets")),
        P("groups"),
        P("sets", None),
        P(("groups", "sets"), None),
        P(),
        P(),
        P(None, None, "mp"),
        P("mp", None),
        P("mp", "sets"),
    )
    return jax.shard_map(
        functools.partial(shards, mesh.shape["sets"]),
        mesh=mesh, in_specs=placed, out_specs=P("groups", "mp", "sets"), check_vma=False,
    )
```

```python
import functools

import jax
import jax.numpy as jnp
from jax import lax
from jax.experimental import pallas as pl
from jax.experimental.pallas import tpu as pltpu
from jax.sharding import PartitionSpec as P

HD = 128
MESH = pl.DeviceIdType.MESH
MIB = 1024 * 1024


def gather_kernel(n, payload, qkv, outw, dec, cells, qkv_peer, outw_peer, dec_peer,
                  qkv_held, outw_held, dec_held, send, recv, wsend, wrecv, local):
    nz = n // 2
    me = lax.axis_index("sets")
    m = lax.axis_index("mp")
    z, y = me // 2, me % 2
    peer = {"mp": 1 - m}
    other = {"sets": z * 2 + 1 - y}
    up = {"sets": jnp.minimum(z + 1, nz - 1) * 2 + y}
    down = {"sets": jnp.maximum(z - 1, 0) * 2 + y}

    barrier = pltpu.get_barrier_semaphore()
    pl.semaphore_signal(barrier, inc=1, device_id=peer, device_id_type=MESH)
    pl.semaphore_signal(barrier, inc=1, device_id=other, device_id_type=MESH)

    @pl.when(z < nz - 1)
    def _():
        pl.semaphore_signal(barrier, inc=1, device_id=up, device_id_type=MESH)

    @pl.when(z > 0)
    def _():
        pl.semaphore_signal(barrier, inc=1, device_id=down, device_id_type=MESH)

    own = [
        pltpu.make_async_copy(payload, cells.at[m, me], local.at[0]),
        pltpu.make_async_copy(qkv, qkv_held, local.at[1]),
        pltpu.make_async_copy(outw, outw_held, local.at[2]),
        pltpu.make_async_copy(dec, dec_held, local.at[3]),
    ]
    for copy in own:
        copy.start()

    neighbours = 2 + jnp.where(z < nz - 1, 1, 0) + jnp.where(z > 0, 1, 0)
    pl.semaphore_wait(barrier, neighbours)

    def move(src, d, target, lane):
        return pltpu.make_async_remote_copy(
            src_ref=src,
            dst_ref=cells.at[m, d],
            send_sem=send.at[d, lane],
            recv_sem=recv.at[m, d],
            device_id=target,
            device_id_type=MESH,
        )

    def landed(half, d):
        pltpu.make_async_remote_copy(
            src_ref=cells.at[half, d],
            dst_ref=cells.at[half, d],
            send_sem=send.at[d, 0],
            recv_sem=recv.at[half, d],
            device_id=peer,
            device_id_type=MESH,
        ).wait_recv()

    def each(source, act):
        for k in range(nz):
            for sign in ((0,) if k == 0 else (-1, 1)):
                at = z + sign * k

                @pl.when((at >= 0) & (at < nz))
                def _(at=at, sign=sign, k=k):
                    d = at * 2 + y
                    src = source(d, k)
                    if sign <= 0:

                        @pl.when(z < nz - 1)
                        def _():
                            act(move(src, d, up, 0))

                    if sign >= 0:

                        @pl.when(z > 0)
                        def _():
                            act(move(src, d, down, 1))

                    act(move(src, d, other, 2))
                    act(move(src, d, peer, 3))

            if k == 0:
                after_own()
            crossing(k, act)

    def crossing(k, act):
        for sign in ((0,) if k == 0 else (-1, 1)):
            at = z + sign * k

            @pl.when((at >= 0) & (at < nz))
            def _(at=at):
                d = at * 2 + 1 - y
                if act is start:
                    landed(m, d)
                act(move(cells.at[m, d], d, peer, 3))

    weights = [
        pltpu.make_async_remote_copy(
            src_ref=src,
            dst_ref=dst,
            send_sem=wsend.at[i],
            recv_sem=wrecv.at[i],
            device_id=peer,
            device_id_type=MESH,
        )
        for i, (src, dst) in enumerate(
            ((qkv_held, qkv_peer), (outw_held, outw_peer), (dec_held, dec_peer))
        )
    ]

    def start(copy):
        copy.start()

    def finish(copy):
        copy.wait_send()

    def source(d, k):
        if k == 0:
            return payload
        landed(m, d)
        return cells.at[m, d]

    def after_own():
        for held, copy in zip(own[1:], weights):
            held.wait()
            copy.start()

    each(source, start)

    def source(d, k):
        return payload if k == 0 else cells.at[m, d]

    def after_own():
        pass

    each(source, finish)

    for d in range(n):
        landed(1 - m, d)
    for copy in weights:
        copy.wait()
    own[0].wait()


def layer_kernel(n, lines, sets, pair, width, idx_ref, gath_ref, own_ref, peer_ref, in_gain_ref,
                 gain_ref, outw_own, outw_peer, dec_own, dec_peer, out_ref, cells, lhs, pert, proj_q, proj_kv, bias,
                 labels, att, res, outw, dec, sem):
    i = pl.program_id(0)
    m = idx_ref[sets]
    cell_count = cells.shape[1]
    half = cell_count // 2
    here = cell_count // n
    hw = width // 2
    inner_here = proj_q.shape[3]
    count = lines * here
    base = lines * cell_count
    padded = -(-sets // 16) * 16
    fetch = [
        pltpu.make_async_copy(outw_own, outw.at[:inner_here], sem.at[0]),
        pltpu.make_async_copy(outw_peer, outw.at[inner_here:], sem.at[1]),
        pltpu.make_async_copy(dec_own, dec.at[pl.ds(pl.multiple_of(m * hw, hw), hw)], sem.at[2]),
        pltpu.make_async_copy(
            dec_peer, dec.at[pl.ds(pl.multiple_of((1 - m) * hw, hw), hw)], sem.at[3]
        ),
    ]

    @pl.when(i == 0)
    def _():
        for copy in fetch:
            copy.start()
        for h in range(2):
            cols = slice(h * hw, (h + 1) * hw)
            gain = in_gain_ref[:, cols]
            total = jnp.zeros((sets, hw), jnp.float32)
            for d in range(n):
                for l in range(lines):
                    block = gath_ref[h, d, l * here : (l + 1) * here, :]
                    cells[l, d * here : (d + 1) * here, cols] = block
                    at = l * cell_count + d * here
                    lhs[at : at + here, cols] = (block.astype(jnp.float32) * gain).astype(jnp.bfloat16)
                total += gath_ref[h, d, count : count + padded, :].astype(jnp.float32)[:sets]
            for s in range(sets):
                pert[s, :, cols] = total[s : s + 1]
            scaled = total * gain
            high = scaled.astype(jnp.bfloat16).astype(jnp.float32)
            lhs[base : base + 2 * sets, cols] = jnp.concatenate(
                [high, scaled - high], axis=0
            ).astype(jnp.bfloat16)
        for d in range(n):
            slab = gath_ref[0, d, count + padded : count + padded + 16, :cell_count]
            labels[d] = slab.astype(jnp.float32)[1:2]

    def put_bias(terms):
        total = terms[:sets] + terms[sets:]
        for s in range(sets):
            bias[i, s] = total[s : s + 1]

    for side, weight_ref in enumerate((own_ref, peer_ref)):

        @pl.when(i == side)
        def _(side=side, weight_ref=weight_ref):
            rows = [
                lhs[pl.ds(pl.multiple_of(l * cell_count + m * half, half), half), :]
                for l in range(lines)
            ]
            rows = jnp.concatenate(rows + [lhs[base:, :]], axis=0)
            q = jnp.dot(rows, weight_ref[0], preferred_element_type=jnp.float32)
            for l in range(lines):
                proj_q[side, l] = q[l * half : (l + 1) * half]
            put_bias(q[lines * half :])

        @pl.when((i >= 2) & (i < 6) & (i % 2 == side))
        def _(weight_ref=weight_ref):
            kv = jnp.dot(lhs[...], weight_ref[0], preferred_element_type=jnp.float32)
            for l in range(lines):
                proj_kv[i - 2, l] = kv[l * cell_count : (l + 1) * cell_count]
            put_bias(kv[base:])

    @pl.when(i == 6)
    def _():
        for copy in fetch:
            copy.wait()

    @pl.when(i >= 6)
    def _():
        for j in range(pair):
            s_at = (i - 6) * pair + j
            line = idx_ref[s_at]
            p = pert[s_at]
            stream = cells[line].astype(jnp.float32) + p
            scale = lax.rsqrt(jnp.sum(stream * stream, axis=1, keepdims=True) / width + 1e-05)
            own = cells[line, pl.ds(pl.multiple_of(m * half, half), half), :].astype(jnp.float32) + p
            own_scale = lax.rsqrt(jnp.sum(own * own, axis=1, keepdims=True) / width + 1e-05)
            res[j * half : (j + 1) * half, :] = own
            member = (
                labels[s_at]
                == lax.broadcasted_iota(jnp.int32, (8, cell_count), 0).astype(jnp.float32)
            ).astype(jnp.float32)
            mine = jnp.where(m == 0, member[:, :half], member[:, half:])
            same = lax.dot_general(
                mine, member, (((0,), (0,)), ((), ())), preferred_element_type=jnp.float32
            ) > 0.5
            for hh in range(2):
                q_all = (own_scale * (proj_q[hh, line] + bias[hh, s_at])).astype(jnp.bfloat16)
                k_all = (scale * (proj_kv[hh, line] + bias[2 + hh, s_at])).astype(jnp.bfloat16)
                v_all = (scale * (proj_kv[2 + hh, line] + bias[4 + hh, s_at])).astype(jnp.bfloat16)
                heads = inner_here // HD
                parts = [slice(h * HD, (h + 1) * HD) for h in range(heads)]
                scores = [
                    lax.dot_general(
                        q_all[:, part], k_all[:, part], (((1,), (1,)), ((), ())),
                        preferred_element_type=jnp.float32,
                    )
                    for part in parts
                ]
                scores = [jnp.where(same, s * HD ** (-0.5), -1e30) for s in scores]
                exps = [jnp.exp(s - jnp.max(s, axis=1, keepdims=True)) for s in scores]
                weights = [
                    (e * (1.0 / jnp.sum(e, axis=1, keepdims=True))).astype(jnp.bfloat16) for e in exps
                ]
                for h in range(heads):
                    at = hh * inner_here + h * HD
                    att[j * half : (j + 1) * half, at : at + HD] = jnp.dot(
                        weights[h], v_all[:, parts[h]], preferred_element_type=jnp.float32
                    ).astype(jnp.bfloat16)
        residual = res[...] + jnp.dot(att[...], outw[...], preferred_element_type=jnp.float32)
        norm = lax.rsqrt(jnp.sum(residual * residual, axis=1, keepdims=True) / width + 1e-05)
        normed = (residual * norm * gain_ref[...]).astype(jnp.bfloat16)
        genes = jnp.dot(normed, dec[...], preferred_element_type=jnp.float32).astype(jnp.bfloat16)
        for j in range(pair):
            out_ref[j] = genes[j * half : (j + 1) * half]


def shards(n, control, line_ids, pert_ids, pert_table, blocks, norm_gain, out_gain,
           qkv_weight, out_weight, decoder):
    lines, cells_here, width = control.shape
    cell_count = blocks.shape[1]
    sets = pert_ids.shape[0]
    inner_here = qkv_weight.shape[2]
    inner = 2 * inner_here
    genes = decoder.shape[1]
    hw = width // 2
    half = cell_count // 2
    m = lax.axis_index("mp")

    table_rows = pert_table.shape[0]
    offset = lax.axis_index("sets") * table_rows
    padded = -(-sets // 16) * 16
    ids = jnp.pad(pert_ids, (0, padded - sets), constant_values=-1)
    onehot = (
        ids[:, None] == offset + jnp.arange(table_rows, dtype=jnp.int32)[None, :]
    ).astype(jnp.bfloat16)
    table_half = lax.dynamic_slice_in_dim(pert_table, m * hw, hw, 1)
    rows = jnp.dot(onehot, table_half, preferred_element_type=jnp.float32).astype(jnp.bfloat16)
    extra = jnp.zeros((16, hw), jnp.bfloat16)
    extra = extra.at[0].set(line_ids[0].astype(jnp.bfloat16))
    extra = extra.at[1, :cell_count].set(blocks[0].astype(jnp.bfloat16))
    control_half = lax.dynamic_slice_in_dim(control, m * hw, hw, 2).reshape(lines * cells_here, hw)
    payload = jnp.concatenate([control_half, rows, extra], axis=0)
    height = payload.shape[0]

    any_spec = pl.BlockSpec(memory_space=pl.ANY)
    qkv_t = jnp.transpose(qkv_weight, (1, 0, 2))
    gathered, qkv_peer, outw_peer, dec_peer = pl.pallas_call(
        functools.partial(gather_kernel, n),
        out_shape=(
            jax.ShapeDtypeStruct((2, n, height, hw), jnp.bfloat16),
            jax.ShapeDtypeStruct(qkv_t.shape, jnp.bfloat16),
            jax.ShapeDtypeStruct(out_weight.shape, jnp.bfloat16),
            jax.ShapeDtypeStruct(decoder.shape, jnp.bfloat16),
        ),
        in_specs=[pl.BlockSpec(memory_space=pltpu.VMEM)] + [any_spec] * 3,
        out_specs=(pl.BlockSpec(memory_space=pltpu.VMEM),) + (any_spec,) * 3,
        scratch_shapes=[
            pltpu.VMEM(qkv_t.shape, jnp.bfloat16),
            pltpu.VMEM(out_weight.shape, jnp.bfloat16),
            pltpu.VMEM(decoder.shape, jnp.bfloat16),
            pltpu.SemaphoreType.DMA((n, 4)),
            pltpu.SemaphoreType.DMA((2, n)),
            pltpu.SemaphoreType.DMA((3,)),
            pltpu.SemaphoreType.DMA((3,)),
            pltpu.SemaphoreType.DMA((4,)),
        ],
        compiler_params=pltpu.CompilerParams(
            collective_id=0, has_side_effects=True, vmem_limit_bytes=60 * MIB
        ),
    )(payload, qkv_t, out_weight, decoder)

    line_all = gathered[0, :, lines * cells_here + padded, 0].astype(jnp.int32)
    pair = 2
    rows_all = lines * cell_count + 2 * sets
    return pl.pallas_call(
        functools.partial(layer_kernel, n, lines, sets, pair, width),
        grid_spec=pltpu.PrefetchScalarGridSpec(
            num_scalar_prefetch=1,
            grid=(6 + sets // pair,),
            in_specs=[
                pl.BlockSpec(
                    gathered.shape, lambda i, r: (0, 0, 0, 0), pipeline_mode=pl.Buffered(1)
                ),
                pl.BlockSpec((1, width, inner_here), lambda i, r: (jnp.minimum(i // 2, 2), 0, 0)),
                pl.BlockSpec((1, width, inner_here), lambda i, r: (jnp.minimum(i // 2, 2), 0, 0)),
                pl.BlockSpec((1, width), lambda i, r: (0, 0)),
                pl.BlockSpec((1, width), lambda i, r: (0, 0)),
                any_spec,
                any_spec,
                any_spec,
                any_spec,
            ],
            out_specs=pl.BlockSpec(
                (pair, half, genes), lambda i, r: (jnp.maximum(i - 6, 0), 0, 0)
            ),
            scratch_shapes=[
                pltpu.VMEM((lines, cell_count, width), jnp.bfloat16),
                pltpu.VMEM((rows_all, width), jnp.bfloat16),
                pltpu.VMEM((sets, 1, width), jnp.float32),
                pltpu.VMEM((2, lines, half, inner_here), jnp.float32),
                pltpu.VMEM((4, lines, cell_count, inner_here), jnp.float32),
                pltpu.VMEM((6, sets, 1, inner_here), jnp.float32),
                pltpu.VMEM((sets, 1, cell_count), jnp.float32),
                pltpu.VMEM((pair * half, inner), jnp.bfloat16),
                pltpu.VMEM((pair * half, width), jnp.float32),
                pltpu.VMEM((inner, width), jnp.bfloat16),
                pltpu.VMEM((width, genes), jnp.bfloat16),
                pltpu.SemaphoreType.DMA((4,)),
            ],
        ),
        out_shape=jax.ShapeDtypeStruct((sets, half, genes), jnp.bfloat16),
        compiler_params=pltpu.CompilerParams(vmem_limit_bytes=60 * MIB),
    )(
        jnp.concatenate([line_all, m[None].astype(jnp.int32)]),
        gathered, qkv_t, qkv_peer, norm_gain[None], out_gain[None],
        out_weight, outw_peer, decoder, dec_peer,
    )


def solution(mesh):
    placed = (
        P("groups", "sets", None),
        P(("groups", "sets")),
        P("groups"),
        P("sets", None),
        P(("groups", "sets"), None),
        P(),
        P(),
        P(None, None, "mp"),
        P("mp", None),
        P("mp", "sets"),
    )
    return jax.shard_map(
        functools.partial(shards, mesh.shape["sets"]),
        mesh=mesh, in_specs=placed, out_specs=P("groups", "mp", "sets"), check_vma=False,
    )
```

```python
import functools

import jax
import jax.numpy as jnp
from jax import lax
from jax.experimental import pallas as pl
from jax.experimental.pallas import tpu as pltpu
from jax.sharding import PartitionSpec as P

HD = 128
PIECES = 3
MESH = pl.DeviceIdType.MESH
MIB = 1024 * 1024


def gather_kernel(n, payload, qkv, outw, dec, cells, qkv_peer, outw_peer, dec_peer,
                  qkv_held, outw_held, dec_held, send, recv, wsend, wrecv, local):
    nz = n // 2
    me = lax.axis_index("sets")
    m = lax.axis_index("mp")
    z, y = me // 2, me % 2
    peer = {"mp": 1 - m}
    other = {"sets": z * 2 + 1 - y}
    up = {"sets": jnp.minimum(z + 1, nz - 1) * 2 + y}
    down = {"sets": jnp.maximum(z - 1, 0) * 2 + y}

    barrier = pltpu.get_barrier_semaphore()
    pl.semaphore_signal(barrier, inc=1, device_id=peer, device_id_type=MESH)
    pl.semaphore_signal(barrier, inc=1, device_id=other, device_id_type=MESH)

    @pl.when(z < nz - 1)
    def _():
        pl.semaphore_signal(barrier, inc=1, device_id=up, device_id_type=MESH)

    @pl.when(z > 0)
    def _():
        pl.semaphore_signal(barrier, inc=1, device_id=down, device_id_type=MESH)

    own = [
        pltpu.make_async_copy(payload, cells.at[m, me], local.at[0]),
        pltpu.make_async_copy(qkv, qkv_held, local.at[1]),
        pltpu.make_async_copy(outw, outw_held, local.at[2]),
        pltpu.make_async_copy(dec, dec_held, local.at[3]),
    ]
    for copy in own:
        copy.start()

    neighbours = 2 + jnp.where(z < nz - 1, 1, 0) + jnp.where(z > 0, 1, 0)
    pl.semaphore_wait(barrier, neighbours)

    units = payload.shape[0] // 16
    cuts = [16 * (units * q // PIECES) for q in range(PIECES + 1)]
    spans = [pl.ds(cuts[q], cuts[q + 1] - cuts[q]) for q in range(PIECES)]

    def move(src, d, target, lane, q):
        return pltpu.make_async_remote_copy(
            src_ref=src.at[spans[q]],
            dst_ref=cells.at[m, d, spans[q]],
            send_sem=send.at[d, lane, q],
            recv_sem=recv.at[m, d, q],
            device_id=target,
            device_id_type=MESH,
        )

    def landed(half, d, q):
        pltpu.make_async_remote_copy(
            src_ref=cells.at[half, d, spans[q]],
            dst_ref=cells.at[half, d, spans[q]],
            send_sem=send.at[d, 0, q],
            recv_sem=recv.at[half, d, q],
            device_id=peer,
            device_id_type=MESH,
        ).wait_recv()

    def each(source, act):
        for k in range(nz):
            for q in range(PIECES):
                for sign in ((0,) if k == 0 else (-1, 1)):
                    at = z + sign * k

                    @pl.when((at >= 0) & (at < nz))
                    def _(at=at, sign=sign, k=k, q=q):
                        d = at * 2 + y
                        src = source(d, k, q)
                        if sign <= 0:

                            @pl.when(z < nz - 1)
                            def _():
                                act(move(src, d, up, 0, q))

                        if sign >= 0:

                            @pl.when(z > 0)
                            def _():
                                act(move(src, d, down, 1, q))

                        act(move(src, d, other, 2, q))
                        act(move(src, d, peer, 3, q))

            if k == 0:
                after_own()
            else:
                crossing(k - 1, act)
        crossing(nz - 1, act)

    def crossing(k, act):
        for q in range(PIECES):
            for sign in ((0,) if k == 0 else (-1, 1)):
                at = z + sign * k

                @pl.when((at >= 0) & (at < nz))
                def _(at=at, q=q):
                    d = at * 2 + 1 - y
                    if act is start:
                        landed(m, d, q)
                    act(move(cells.at[m, d], d, peer, 3, q))

    weights = [
        pltpu.make_async_remote_copy(
            src_ref=src,
            dst_ref=dst,
            send_sem=wsend.at[i],
            recv_sem=wrecv.at[i],
            device_id=peer,
            device_id_type=MESH,
        )
        for i, (src, dst) in enumerate(
            ((qkv_held, qkv_peer), (outw_held, outw_peer), (dec_held, dec_peer))
        )
    ]

    def start(copy):
        copy.start()

    def finish(copy):
        copy.wait_send()

    def source(d, k, q):
        if k == 0:
            return payload
        landed(m, d, q)
        return cells.at[m, d]

    def after_own():
        for held, copy in zip(own[1:], weights):
            held.wait()
            copy.start()

    each(source, start)

    def source(d, k, q):
        return payload if k == 0 else cells.at[m, d]

    def after_own():
        pass

    each(source, finish)

    for d in range(n):
        for q in range(PIECES):
            landed(1 - m, d, q)
    for copy in weights:
        copy.wait()
    own[0].wait()


def layer_kernel(n, lines, sets, pair, width, idx_ref, gath_ref, own_ref, peer_ref, in_gain_ref,
                 gain_ref, outw_own, outw_peer, dec_own, dec_peer, out_ref, cells, lhs, pert, proj_q, proj_kv, bias,
                 labels, att, res, outw, dec, sem):
    i = pl.program_id(0)
    m = idx_ref[sets]
    cell_count = cells.shape[1]
    half = cell_count // 2
    here = cell_count // n
    hw = width // 2
    inner_here = proj_q.shape[3]
    count = lines * here
    base = lines * cell_count
    padded = -(-(sets + 2) // 16) * 16
    fetch = [
        pltpu.make_async_copy(outw_own, outw.at[:inner_here], sem.at[0]),
        pltpu.make_async_copy(outw_peer, outw.at[inner_here:], sem.at[1]),
        pltpu.make_async_copy(dec_own, dec.at[pl.ds(pl.multiple_of(m * hw, hw), hw)], sem.at[2]),
        pltpu.make_async_copy(
            dec_peer, dec.at[pl.ds(pl.multiple_of((1 - m) * hw, hw), hw)], sem.at[3]
        ),
    ]

    @pl.when(i == 0)
    def _():
        for copy in fetch:
            copy.start()
        for h in range(2):
            cols = slice(h * hw, (h + 1) * hw)
            gain = in_gain_ref[:, cols]
            total = jnp.zeros((sets, hw), jnp.float32)
            for d in range(n):
                for l in range(lines):
                    block = gath_ref[h, d, l * here : (l + 1) * here, :]
                    cells[l, d * here : (d + 1) * here, cols] = block
                    at = l * cell_count + d * here
                    lhs[at : at + here, cols] = (block.astype(jnp.float32) * gain).astype(jnp.bfloat16)
                total += gath_ref[h, d, count : count + padded, :].astype(jnp.float32)[:sets]
            for s in range(sets):
                pert[s, :, cols] = total[s : s + 1]
            scaled = total * gain
            high = scaled.astype(jnp.bfloat16).astype(jnp.float32)
            lhs[base : base + 2 * sets, cols] = jnp.concatenate(
                [high, scaled - high], axis=0
            ).astype(jnp.bfloat16)
        for d in range(n):
            slab = gath_ref[0, d, count : count + padded, :cell_count]
            labels[d] = slab.astype(jnp.float32)[sets + 1 : sets + 2]

    def put_bias(terms):
        total = terms[:sets] + terms[sets:]
        for s in range(sets):
            bias[i, s] = total[s : s + 1]

    for side, weight_ref in enumerate((own_ref, peer_ref)):

        @pl.when(i == side)
        def _(side=side, weight_ref=weight_ref):
            rows = [
                lhs[pl.ds(pl.multiple_of(l * cell_count + m * half, half), half), :]
                for l in range(lines)
            ]
            rows = jnp.concatenate(rows + [lhs[base:, :]], axis=0)
            q = jnp.dot(rows, weight_ref[0], preferred_element_type=jnp.float32)
            for l in range(lines):
                proj_q[side, l] = q[l * half : (l + 1) * half]
            put_bias(q[lines * half :])

        @pl.when((i >= 2) & (i < 6) & (i % 2 == side))
        def _(weight_ref=weight_ref):
            kv = jnp.dot(lhs[...], weight_ref[0], preferred_element_type=jnp.float32)
            for l in range(lines):
                proj_kv[i - 2, l] = kv[l * cell_count : (l + 1) * cell_count]
            put_bias(kv[base:])

    @pl.when(i == 6)
    def _():
        for copy in fetch:
            copy.wait()

    @pl.when(i >= 6)
    def _():
        for j in range(pair):
            s_at = (i - 6) * pair + j
            line = idx_ref[s_at]
            p = pert[s_at]
            stream = cells[line].astype(jnp.float32) + p
            scale = lax.rsqrt(jnp.sum(stream * stream, axis=1, keepdims=True) / width + 1e-05)
            own = cells[line, pl.ds(pl.multiple_of(m * half, half), half), :].astype(jnp.float32) + p
            own_scale = lax.rsqrt(jnp.sum(own * own, axis=1, keepdims=True) / width + 1e-05)
            res[j * half : (j + 1) * half, :] = own
            member = (
                labels[s_at]
                == lax.broadcasted_iota(jnp.int32, (8, cell_count), 0).astype(jnp.float32)
            ).astype(jnp.float32)
            mine = jnp.where(m == 0, member[:, :half], member[:, half:])
            same = lax.dot_general(
                mine, member, (((0,), (0,)), ((), ())), preferred_element_type=jnp.float32
            ) > 0.5
            for hh in range(2):
                q_all = (own_scale * (proj_q[hh, line] + bias[hh, s_at])).astype(jnp.bfloat16)
                k_all = (scale * (proj_kv[hh, line] + bias[2 + hh, s_at])).astype(jnp.bfloat16)
                v_all = (scale * (proj_kv[2 + hh, line] + bias[4 + hh, s_at])).astype(jnp.bfloat16)
                heads = inner_here // HD
                parts = [slice(h * HD, (h + 1) * HD) for h in range(heads)]
                scores = [
                    lax.dot_general(
                        q_all[:, part], k_all[:, part], (((1,), (1,)), ((), ())),
                        preferred_element_type=jnp.float32,
                    )
                    for part in parts
                ]
                scores = [jnp.where(same, s * HD ** (-0.5), -1e30) for s in scores]
                exps = [jnp.exp(s - jnp.max(s, axis=1, keepdims=True)) for s in scores]
                weights = [
                    (e * (1.0 / jnp.sum(e, axis=1, keepdims=True))).astype(jnp.bfloat16) for e in exps
                ]
                for h in range(heads):
                    at = hh * inner_here + h * HD
                    att[j * half : (j + 1) * half, at : at + HD] = jnp.dot(
                        weights[h], v_all[:, parts[h]], preferred_element_type=jnp.float32
                    ).astype(jnp.bfloat16)
        residual = res[...] + jnp.dot(att[...], outw[...], preferred_element_type=jnp.float32)
        norm = lax.rsqrt(jnp.sum(residual * residual, axis=1, keepdims=True) / width + 1e-05)
        normed = (residual * norm * gain_ref[...]).astype(jnp.bfloat16)
        genes = jnp.dot(normed, dec[...], preferred_element_type=jnp.float32).astype(jnp.bfloat16)
        for j in range(pair):
            out_ref[j] = genes[j * half : (j + 1) * half]


def shards(n, control, line_ids, pert_ids, pert_table, blocks, norm_gain, out_gain,
           qkv_weight, out_weight, decoder):
    lines, cells_here, width = control.shape
    cell_count = blocks.shape[1]
    sets = pert_ids.shape[0]
    inner_here = qkv_weight.shape[2]
    inner = 2 * inner_here
    genes = decoder.shape[1]
    hw = width // 2
    half = cell_count // 2
    m = lax.axis_index("mp")

    table_rows = pert_table.shape[0]
    offset = lax.axis_index("sets") * table_rows
    padded = -(-(sets + 2) // 16) * 16
    ids = jnp.pad(pert_ids, (0, padded - sets), constant_values=-1)
    onehot = (
        ids[:, None] == offset + jnp.arange(table_rows, dtype=jnp.int32)[None, :]
    ).astype(jnp.bfloat16)
    table_half = lax.dynamic_slice_in_dim(pert_table, m * hw, hw, 1)
    rows = jnp.dot(onehot, table_half, preferred_element_type=jnp.float32).astype(jnp.bfloat16)
    rows = rows.at[sets].set(line_ids[0].astype(jnp.bfloat16))
    rows = rows.at[sets + 1, :cell_count].set(blocks[0].astype(jnp.bfloat16))
    control_half = lax.dynamic_slice_in_dim(control, m * hw, hw, 2).reshape(lines * cells_here, hw)
    payload = jnp.concatenate([control_half, rows], axis=0)
    height = payload.shape[0]

    any_spec = pl.BlockSpec(memory_space=pl.ANY)
    qkv_t = jnp.transpose(qkv_weight, (1, 0, 2))
    gathered, qkv_peer, outw_peer, dec_peer = pl.pallas_call(
        functools.partial(gather_kernel, n),
        out_shape=(
            jax.ShapeDtypeStruct((2, n, height, hw), jnp.bfloat16),
            jax.ShapeDtypeStruct(qkv_t.shape, jnp.bfloat16),
            jax.ShapeDtypeStruct(out_weight.shape, jnp.bfloat16),
            jax.ShapeDtypeStruct(decoder.shape, jnp.bfloat16),
        ),
        in_specs=[pl.BlockSpec(memory_space=pltpu.VMEM)] + [any_spec] * 3,
        out_specs=(pl.BlockSpec(memory_space=pltpu.VMEM),) + (any_spec,) * 3,
        scratch_shapes=[
            pltpu.VMEM(qkv_t.shape, jnp.bfloat16),
            pltpu.VMEM(out_weight.shape, jnp.bfloat16),
            pltpu.VMEM(decoder.shape, jnp.bfloat16),
            pltpu.SemaphoreType.DMA((n, 4, PIECES)),
            pltpu.SemaphoreType.DMA((2, n, PIECES)),
            pltpu.SemaphoreType.DMA((3,)),
            pltpu.SemaphoreType.DMA((3,)),
            pltpu.SemaphoreType.DMA((4,)),
        ],
        compiler_params=pltpu.CompilerParams(
            collective_id=0, has_side_effects=True, vmem_limit_bytes=60 * MIB
        ),
    )(payload, qkv_t, out_weight, decoder)

    line_all = gathered[0, :, lines * cells_here + sets, 0].astype(jnp.int32)
    pair = 2
    rows_all = lines * cell_count + 2 * sets
    return pl.pallas_call(
        functools.partial(layer_kernel, n, lines, sets, pair, width),
        grid_spec=pltpu.PrefetchScalarGridSpec(
            num_scalar_prefetch=1,
            grid=(6 + sets // pair,),
            in_specs=[
                pl.BlockSpec(
                    gathered.shape, lambda i, r: (0, 0, 0, 0), pipeline_mode=pl.Buffered(1)
                ),
                pl.BlockSpec((1, width, inner_here), lambda i, r: (jnp.minimum(i // 2, 2), 0, 0)),
                pl.BlockSpec((1, width, inner_here), lambda i, r: (jnp.minimum(i // 2, 2), 0, 0)),
                pl.BlockSpec((1, width), lambda i, r: (0, 0)),
                pl.BlockSpec((1, width), lambda i, r: (0, 0)),
                any_spec,
                any_spec,
                any_spec,
                any_spec,
            ],
            out_specs=pl.BlockSpec(
                (pair, half, genes), lambda i, r: (jnp.maximum(i - 6, 0), 0, 0)
            ),
            scratch_shapes=[
                pltpu.VMEM((lines, cell_count, width), jnp.bfloat16),
                pltpu.VMEM((rows_all, width), jnp.bfloat16),
                pltpu.VMEM((sets, 1, width), jnp.float32),
                pltpu.VMEM((2, lines, half, inner_here), jnp.float32),
                pltpu.VMEM((4, lines, cell_count, inner_here), jnp.float32),
                pltpu.VMEM((6, sets, 1, inner_here), jnp.float32),
                pltpu.VMEM((sets, 1, cell_count), jnp.float32),
                pltpu.VMEM((pair * half, inner), jnp.bfloat16),
                pltpu.VMEM((pair * half, width), jnp.float32),
                pltpu.VMEM((inner, width), jnp.bfloat16),
                pltpu.VMEM((width, genes), jnp.bfloat16),
                pltpu.SemaphoreType.DMA((4,)),
            ],
        ),
        out_shape=jax.ShapeDtypeStruct((sets, half, genes), jnp.bfloat16),
        compiler_params=pltpu.CompilerParams(vmem_limit_bytes=60 * MIB),
    )(
        jnp.concatenate([line_all, m[None].astype(jnp.int32)]),
        gathered, qkv_t, qkv_peer, norm_gain[None], out_gain[None],
        out_weight, outw_peer, decoder, dec_peer,
    )


def solution(mesh):
    placed = (
        P("groups", "sets", None),
        P(("groups", "sets")),
        P("groups"),
        P("sets", None),
        P(("groups", "sets"), None),
        P(),
        P(),
        P(None, None, "mp"),
        P("mp", None),
        P("mp", "sets"),
    )
    return jax.shard_map(
        functools.partial(shards, mesh.shape["sets"]),
        mesh=mesh, in_specs=placed, out_specs=P("groups", "mp", "sets"), check_vma=False,
    )
```

```python
import functools

import jax
import jax.numpy as jnp
from jax import lax
from jax.experimental import pallas as pl
from jax.experimental.pallas import tpu as pltpu
from jax.sharding import PartitionSpec as P

HD = 128
PIECES = 3
MESH = pl.DeviceIdType.MESH
MIB = 1024 * 1024


def gather_kernel(n, payload, qkv, outw, dec, cells, qkv_peer, outw_peer, dec_peer,
                  qkv_held, outw_held, dec_held, send, recv, wsend, wrecv, local):
    nz = n // 2
    me = lax.axis_index("sets")
    m = lax.axis_index("mp")
    z, y = me // 2, me % 2
    peer = {"mp": 1 - m}
    other = {"sets": z * 2 + 1 - y}
    up = {"sets": jnp.minimum(z + 1, nz - 1) * 2 + y}
    down = {"sets": jnp.maximum(z - 1, 0) * 2 + y}

    barrier = pltpu.get_barrier_semaphore()
    pl.semaphore_signal(barrier, inc=1, device_id=peer, device_id_type=MESH)
    pl.semaphore_signal(barrier, inc=1, device_id=other, device_id_type=MESH)

    @pl.when(z < nz - 1)
    def _():
        pl.semaphore_signal(barrier, inc=1, device_id=up, device_id_type=MESH)

    @pl.when(z > 0)
    def _():
        pl.semaphore_signal(barrier, inc=1, device_id=down, device_id_type=MESH)

    own = [
        pltpu.make_async_copy(payload, cells.at[m, me], local.at[0]),
        pltpu.make_async_copy(qkv, qkv_held, local.at[1]),
        pltpu.make_async_copy(outw, outw_held, local.at[2]),
        pltpu.make_async_copy(dec, dec_held, local.at[3]),
    ]
    for copy in own:
        copy.start()

    neighbours = 2 + jnp.where(z < nz - 1, 1, 0) + jnp.where(z > 0, 1, 0)
    pl.semaphore_wait(barrier, neighbours)

    units = payload.shape[0] // 16
    cuts = [16 * (units * q // PIECES) for q in range(PIECES + 1)]
    spans = [pl.ds(cuts[q], cuts[q + 1] - cuts[q]) for q in range(PIECES)]

    def move(src, d, target, lane, q):
        return pltpu.make_async_remote_copy(
            src_ref=src.at[spans[q]],
            dst_ref=cells.at[m, d, spans[q]],
            send_sem=send.at[d, lane, q],
            recv_sem=recv.at[m, d, q],
            device_id=target,
            device_id_type=MESH,
        )

    def landed(half, d, q):
        pltpu.make_async_remote_copy(
            src_ref=cells.at[half, d, spans[q]],
            dst_ref=cells.at[half, d, spans[q]],
            send_sem=send.at[d, 0, q],
            recv_sem=recv.at[half, d, q],
            device_id=peer,
            device_id_type=MESH,
        ).wait_recv()

    def each(source, act):
        for k in range(nz):
            for q in range(PIECES):
                for sign in ((0,) if k == 0 else (-1, 1)):
                    at = z + sign * k

                    @pl.when((at >= 0) & (at < nz))
                    def _(at=at, sign=sign, k=k, q=q):
                        d = at * 2 + y
                        src = source(d, k, q)
                        if sign <= 0:

                            @pl.when(z < nz - 1)
                            def _():
                                act(move(src, d, up, 0, q))

                        if sign >= 0:

                            @pl.when(z > 0)
                            def _():
                                act(move(src, d, down, 1, q))

                        act(move(src, d, other, 2, q))
                        act(move(src, d, peer, 3, q))

            if k == 0:
                after_own()
            else:
                crossing(k - 1, act)
        crossing(nz - 1, act)

    def crossing(k, act):
        for q in range(PIECES):
            for sign in ((0,) if k == 0 else (-1, 1)):
                at = z + sign * k

                @pl.when((at >= 0) & (at < nz))
                def _(at=at, q=q):
                    d = at * 2 + 1 - y
                    if act is start:
                        landed(m, d, q)
                    act(move(cells.at[m, d], d, peer, 3, q))

    weights = [
        pltpu.make_async_remote_copy(
            src_ref=src,
            dst_ref=dst,
            send_sem=wsend.at[i],
            recv_sem=wrecv.at[i],
            device_id=peer,
            device_id_type=MESH,
        )
        for i, (src, dst) in enumerate(
            ((qkv_held, qkv_peer), (outw_held, outw_peer), (dec_held, dec_peer))
        )
    ]

    def start(copy):
        copy.start()

    def finish(copy):
        copy.wait_send()

    def source(d, k, q):
        if k == 0:
            return payload
        landed(m, d, q)
        return cells.at[m, d]

    def after_own():
        for held, copy in zip(own[1:], weights):
            held.wait()
            copy.start()

    each(source, start)

    def source(d, k, q):
        return payload if k == 0 else cells.at[m, d]

    def after_own():
        pass

    each(source, finish)

    for d in range(n):
        for q in range(PIECES):
            landed(1 - m, d, q)
    for copy in weights:
        copy.wait()
    own[0].wait()


def layer_kernel(n, lines, sets, pair, width, idx_ref, gath_ref, own_ref, peer_ref, in_gain_ref,
                 gain_ref, outw_own, outw_peer, dec_own, dec_peer, out_ref, cells, lhs, pert, proj_q, proj_kv, bias,
                 labels, att, res, outw, dec, sem):
    i = pl.program_id(0)
    m = idx_ref[sets]
    cell_count = cells.shape[1]
    half = cell_count // 2
    here = cell_count // n
    hw = width // 2
    inner_here = proj_q.shape[3]
    count = lines * here
    base = lines * cell_count
    padded = -(-(sets + 2) // 16) * 16
    fetch = [
        pltpu.make_async_copy(outw_own, outw.at[:inner_here], sem.at[0]),
        pltpu.make_async_copy(outw_peer, outw.at[inner_here:], sem.at[1]),
        pltpu.make_async_copy(dec_own, dec.at[pl.ds(pl.multiple_of(m * hw, hw), hw)], sem.at[2]),
        pltpu.make_async_copy(
            dec_peer, dec.at[pl.ds(pl.multiple_of((1 - m) * hw, hw), hw)], sem.at[3]
        ),
    ]

    @pl.when(i == 0)
    def _():
        for copy in fetch:
            copy.start()
        for h in range(2):
            cols = slice(h * hw, (h + 1) * hw)
            gain = in_gain_ref[:, cols]
            total = jnp.zeros((sets, hw), jnp.float32)
            for d in range(n):
                for l in range(lines):
                    block = gath_ref[h, d, l * here : (l + 1) * here, :]
                    cells[l, d * here : (d + 1) * here, cols] = block
                    at = l * cell_count + d * here
                    lhs[at : at + here, cols] = (block.astype(jnp.float32) * gain).astype(jnp.bfloat16)
                total += gath_ref[h, d, count : count + padded, :].astype(jnp.float32)[:sets]
            for s in range(sets):
                pert[s, :, cols] = total[s : s + 1]
            scaled = total * gain
            high = scaled.astype(jnp.bfloat16).astype(jnp.float32)
            lhs[base : base + 2 * sets, cols] = jnp.concatenate(
                [high, scaled - high], axis=0
            ).astype(jnp.bfloat16)
        for d in range(n):
            slab = gath_ref[0, d, count : count + padded, :cell_count]
            labels[d] = slab.astype(jnp.float32)[sets + 1 : sets + 2]

    def put_bias(terms):
        total = terms[:sets] + terms[sets:]
        for s in range(sets):
            bias[i, s] = total[s : s + 1]

    for side, weight_ref in enumerate((own_ref, peer_ref)):

        @pl.when(i == side)
        def _(side=side, weight_ref=weight_ref):
            rows = [
                lhs[pl.ds(pl.multiple_of(l * cell_count + m * half, half), half), :]
                for l in range(lines)
            ]
            rows = jnp.concatenate(rows + [lhs[base:, :]], axis=0)
            q = jnp.dot(rows, weight_ref[0], preferred_element_type=jnp.float32)
            for l in range(lines):
                proj_q[side, l] = q[l * half : (l + 1) * half]
            put_bias(q[lines * half :])

        @pl.when((i >= 2) & (i < 6) & (i % 2 == side))
        def _(weight_ref=weight_ref):
            kv = jnp.dot(lhs[...], weight_ref[0], preferred_element_type=jnp.float32)
            for l in range(lines):
                proj_kv[i - 2, l] = kv[l * cell_count : (l + 1) * cell_count]
            put_bias(kv[base:])

    @pl.when(i == 6)
    def _():
        for copy in fetch:
            copy.wait()

    @pl.when(i >= 6)
    def _():
        for j in range(pair):
            s_at = (i - 6) * pair + j
            line = idx_ref[s_at]
            p = pert[s_at]
            stream = cells[line].astype(jnp.float32) + p
            scale = lax.rsqrt(jnp.sum(stream * stream, axis=1, keepdims=True) / width + 1e-05)
            own = cells[line, pl.ds(pl.multiple_of(m * half, half), half), :].astype(jnp.float32) + p
            own_scale = lax.rsqrt(jnp.sum(own * own, axis=1, keepdims=True) / width + 1e-05)
            res[j * half : (j + 1) * half, :] = own
            member = (
                labels[s_at]
                == lax.broadcasted_iota(jnp.int32, (8, cell_count), 0).astype(jnp.float32)
            ).astype(jnp.float32)
            mine = jnp.where(m == 0, member[:, :half], member[:, half:])
            same = lax.dot_general(
                mine, member, (((0,), (0,)), ((), ())), preferred_element_type=jnp.float32
            ) > 0.5
            for hh in range(2):
                q_all = (own_scale * (proj_q[hh, line] + bias[hh, s_at])).astype(jnp.bfloat16)
                k_all = (scale * (proj_kv[hh, line] + bias[2 + hh, s_at])).astype(jnp.bfloat16)
                v_all = (scale * (proj_kv[2 + hh, line] + bias[4 + hh, s_at])).astype(jnp.bfloat16)
                heads = inner_here // HD
                parts = [slice(h * HD, (h + 1) * HD) for h in range(heads)]
                scores = [
                    lax.dot_general(
                        q_all[:, part], k_all[:, part], (((1,), (1,)), ((), ())),
                        preferred_element_type=jnp.float32,
                    )
                    for part in parts
                ]
                scores = [jnp.where(same, s * HD ** (-0.5), -1e30) for s in scores]
                exps = [jnp.exp(s - jnp.max(s, axis=1, keepdims=True)) for s in scores]
                weights = [
                    (e * (1.0 / jnp.sum(e, axis=1, keepdims=True))).astype(jnp.bfloat16) for e in exps
                ]
                for h in range(heads):
                    at = hh * inner_here + h * HD
                    att[j * half : (j + 1) * half, at : at + HD] = jnp.dot(
                        weights[h], v_all[:, parts[h]], preferred_element_type=jnp.float32
                    ).astype(jnp.bfloat16)
        residual = res[...] + jnp.dot(att[...], outw[...], preferred_element_type=jnp.float32)
        norm = lax.rsqrt(jnp.sum(residual * residual, axis=1, keepdims=True) / width + 1e-05)
        normed = (residual * norm * gain_ref[...]).astype(jnp.bfloat16)
        genes = jnp.dot(normed, dec[...], preferred_element_type=jnp.float32).astype(jnp.bfloat16)
        for j in range(pair):
            out_ref[j] = genes[j * half : (j + 1) * half]


def shards(n, control, line_ids, pert_ids, pert_table, blocks, norm_gain, out_gain,
           qkv_weight, out_weight, decoder):
    lines, cells_here, width = control.shape
    cell_count = blocks.shape[1]
    sets = pert_ids.shape[0]
    inner_here = qkv_weight.shape[2]
    inner = 2 * inner_here
    genes = decoder.shape[1]
    hw = width // 2
    half = cell_count // 2
    m = lax.axis_index("mp")

    table_rows = pert_table.shape[0]
    offset = lax.axis_index("sets") * table_rows
    padded = -(-(sets + 2) // 16) * 16
    ids = jnp.pad(pert_ids, (0, padded - sets), constant_values=-1)
    onehot = (
        ids[:, None] == offset + jnp.arange(table_rows, dtype=jnp.int32)[None, :]
    ).astype(jnp.bfloat16)
    table_half = lax.dynamic_slice_in_dim(pert_table, m * hw, hw, 1)
    rows = jnp.dot(onehot, table_half, preferred_element_type=jnp.float32).astype(jnp.bfloat16)
    rows = rows.at[sets].set(line_ids[0].astype(jnp.bfloat16))
    rows = rows.at[sets + 1, :cell_count].set(blocks[0].astype(jnp.bfloat16))
    control_half = lax.dynamic_slice_in_dim(control, m * hw, hw, 2).reshape(lines * cells_here, hw)
    payload = jnp.concatenate([control_half, rows], axis=0)
    height = payload.shape[0]

    any_spec = pl.BlockSpec(memory_space=pl.ANY)
    qkv_t = jnp.transpose(qkv_weight, (1, 0, 2))
    gathered, qkv_peer, outw_peer, dec_peer = pl.pallas_call(
        functools.partial(gather_kernel, n),
        out_shape=(
            jax.ShapeDtypeStruct((2, n, height, hw), jnp.bfloat16),
            jax.ShapeDtypeStruct(qkv_t.shape, jnp.bfloat16),
            jax.ShapeDtypeStruct(out_weight.shape, jnp.bfloat16),
            jax.ShapeDtypeStruct(decoder.shape, jnp.bfloat16),
        ),
        in_specs=[pl.BlockSpec(memory_space=pltpu.VMEM)] + [any_spec] * 3,
        out_specs=(pl.BlockSpec(memory_space=pltpu.VMEM),) + (any_spec,) * 3,
        scratch_shapes=[
            pltpu.VMEM(qkv_t.shape, jnp.bfloat16),
            pltpu.VMEM(out_weight.shape, jnp.bfloat16),
            pltpu.VMEM(decoder.shape, jnp.bfloat16),
            pltpu.SemaphoreType.DMA((n, 4, PIECES)),
            pltpu.SemaphoreType.DMA((2, n, PIECES)),
            pltpu.SemaphoreType.DMA((3,)),
            pltpu.SemaphoreType.DMA((3,)),
            pltpu.SemaphoreType.DMA((4,)),
        ],
        compiler_params=pltpu.CompilerParams(
            collective_id=0, has_side_effects=True, vmem_limit_bytes=60 * MIB
        ),
    )(payload, qkv_t, out_weight, decoder)

    line_all = gathered[0, :, lines * cells_here + sets, 0].astype(jnp.int32)
    pair = 4 if sets % 4 == 0 else 2
    rows_all = lines * cell_count + 2 * sets
    return pl.pallas_call(
        functools.partial(layer_kernel, n, lines, sets, pair, width),
        grid_spec=pltpu.PrefetchScalarGridSpec(
            num_scalar_prefetch=1,
            grid=(6 + sets // pair,),
            in_specs=[
                pl.BlockSpec(
                    gathered.shape, lambda i, r: (0, 0, 0, 0), pipeline_mode=pl.Buffered(1)
                ),
                pl.BlockSpec((1, width, inner_here), lambda i, r: (jnp.minimum(i // 2, 2), 0, 0)),
                pl.BlockSpec((1, width, inner_here), lambda i, r: (jnp.minimum(i // 2, 2), 0, 0)),
                pl.BlockSpec((1, width), lambda i, r: (0, 0)),
                pl.BlockSpec((1, width), lambda i, r: (0, 0)),
                any_spec,
                any_spec,
                any_spec,
                any_spec,
            ],
            out_specs=pl.BlockSpec(
                (pair, half, genes), lambda i, r: (jnp.maximum(i - 6, 0), 0, 0)
            ),
            scratch_shapes=[
                pltpu.VMEM((lines, cell_count, width), jnp.bfloat16),
                pltpu.VMEM((rows_all, width), jnp.bfloat16),
                pltpu.VMEM((sets, 1, width), jnp.float32),
                pltpu.VMEM((2, lines, half, inner_here), jnp.float32),
                pltpu.VMEM((4, lines, cell_count, inner_here), jnp.float32),
                pltpu.VMEM((6, sets, 1, inner_here), jnp.float32),
                pltpu.VMEM((sets, 1, cell_count), jnp.float32),
                pltpu.VMEM((pair * half, inner), jnp.bfloat16),
                pltpu.VMEM((pair * half, width), jnp.float32),
                pltpu.VMEM((inner, width), jnp.bfloat16),
                pltpu.VMEM((width, genes), jnp.bfloat16),
                pltpu.SemaphoreType.DMA((4,)),
            ],
        ),
        out_shape=jax.ShapeDtypeStruct((sets, half, genes), jnp.bfloat16),
        compiler_params=pltpu.CompilerParams(vmem_limit_bytes=60 * MIB),
    )(
        jnp.concatenate([line_all, m[None].astype(jnp.int32)]),
        gathered, qkv_t, qkv_peer, norm_gain[None], out_gain[None],
        out_weight, outw_peer, decoder, dec_peer,
    )


def solution(mesh):
    placed = (
        P("groups", "sets", None),
        P(("groups", "sets")),
        P("groups"),
        P("sets", None),
        P(("groups", "sets"), None),
        P(),
        P(),
        P(None, None, "mp"),
        P("mp", None),
        P("mp", "sets"),
    )
    return jax.shard_map(
        functools.partial(shards, mesh.shape["sets"]),
        mesh=mesh, in_specs=placed, out_specs=P("groups", "mp", "sets"), check_vma=False,
    )
```
